32 devices in a mesh: seq: 8 (over z, x), dp: 4 (over y, core).
Axes of the slice: x: 2, y: 2, z: 4, core: 2. Of those that a mesh axis runs over, the one named last changes fastest.
Arguments:
- layer_input: bfloat16 [4, 1024, 4096], P('dp', 'seq'), may hold values from -6 to 6
- query_rows: bfloat16 [4, 1024, 4096], P('dp', 'seq')
- key_rows: bfloat16 [4, 1024, 4096], P('dp', 'seq')
- value_rows: bfloat16 [4, 1024, 4096], P('dp', 'seq'), may hold values from -6 to 6
- out_grad: bfloat16 [4, 1024, 4096], P('dp', 'seq'), may hold values from -6 to 6
- neighbours: int32 [4, 8, 8], P('dp'), may hold values from 0 to 7, as said below
- counts: int32 [4, 8], P('dp'), may hold values from 1 to 8, as said below
Outputs:
- query_grad: bfloat16 [4, 1024, 4096], P('dp', 'seq')
- key_grad: bfloat16 [4, 1024, 4096], P('dp', 'seq')
- value_grad: bfloat16 [4, 1024, 4096], P('dp', 'seq')
- weight_grad: float32 [3, 4096, 4096], P(None, 'dp', 'seq')
The draws below stay inside these ranges and needn't reach their ends.
Inputs may be any that keep to these rules, and one draw needn't show every extreme that they name: `neighbours`: each row lists 8 distinct key blocks of the same snapshot, the query block itself first; entries past counts are not attended. `counts`: every snapshot has a query block with 8.
All inputs are finite; a program needn't handle non-finite values.
Results may differ from the reference program's by a relative error of at most 0.015.
Values may be sent and summed in bfloat16 or wider, within the bound.
No kernel may reach another device: no remote copies, remote signals or barrier semaphores. Data moves between devices by JAX's collectives and lax.ppermute only.
A program may use at most 192 MiB of HBM per device.

```python
import jax
import jax.numpy as jnp
from jax import lax

D = 4096
H = 32
HDIM = 128
BLK = 128
MAXNB = 8
HD = 4096
SNAP_TOK = 1024
SNAPS = 4
NQB = 8
TOKENS = 4096


def shared_keys(key):
    return jax.random.normal(jax.random.fold_in(key, 31), (SNAPS, SNAP_TOK, HD), jnp.float32)


def draw_key_rows(key, part):
    key_base = shared_keys(key)
    return key_base.astype(jnp.bfloat16)


def draw_query_rows(key, part):
    queries = jax.random.normal(jax.random.fold_in(key, 41), (SNAPS, SNAP_TOK, HD), jnp.float32)
    return queries.astype(jnp.bfloat16)


def draw_neighbours(key, part):
    random_part = jax.random.randint(jax.random.fold_in(key, 23), (SNAPS, NQB, NQB), 0, NQB)
    index = jnp.arange(NQB)
    distance = jnp.abs(index[None, None, :] - index[None, :, None])
    ranking = (random_part + 2 * distance) * NQB + index[None, None, :]
    ranking = jnp.where(index[None, None, :] == index[None, :, None], -1, ranking)
    order = jnp.argsort(ranking, axis=-1, stable=True)
    return order[:, :, :MAXNB].astype(jnp.int32)


def draw_counts(key, part):
    ceiling = jax.random.randint(jax.random.fold_in(key, 11), (SNAPS, 1), 2, MAXNB + 1)
    base = jax.random.randint(jax.random.fold_in(key, 13), (SNAPS, NQB), 0, 1 << 20) % ceiling + 1
    fullest = jax.random.randint(jax.random.fold_in(key, 17), (SNAPS, 1), 0, NQB)
    base = jnp.where(jnp.arange(NQB)[None, :] == fullest, MAXNB, base)
    return base.astype(jnp.int32)


def block_scale(rng, extent, cuts, smallest, largest):
    loudness = 1.0
    for axis_at, shards_of in cuts:
        heights = jax.random.uniform(jax.random.fold_in(jax.random.fold_in(rng, 6), axis_at), (shards_of,), jnp.float32, smallest / len(cuts), largest / len(cuts))
        loudness = loudness * jnp.repeat(jnp.exp(heights), extent[axis_at] // shards_of).reshape((-1,) + (1,) * (len(extent) - 1 - axis_at))
    return loudness


def scatter_about(stream_key, extent, width, limit, cuts=(), kind=jnp.bfloat16):
    values = jax.random.normal(stream_key, extent, jnp.float32) * width
    if len(cuts) > 0:
        values = block_scale(stream_key, extent, cuts, -0.22, 0.18) * values
    return jnp.clip(values, min=-limit, max=limit).astype(kind)


def setup_inputs(seed: int = 0) -> dict:
    key_of = jax.random.split(jax.random.key(seed), 8)
    return {
        "layer_input": scatter_about(key_of[0], (SNAPS, SNAP_TOK, D), 1.0, 6.0, ((0, 4), (1, 8))),
        "query_rows": draw_query_rows(jax.random.fold_in(key_of[7], 71), 0),
        "key_rows": draw_key_rows(jax.random.fold_in(key_of[7], 71), 0),
        "value_rows": scatter_about(key_of[3], (SNAPS, SNAP_TOK, HD), 1.0, 6.0, ((0, 4), (1, 8))),
        "out_grad": scatter_about(key_of[4], (SNAPS, SNAP_TOK, HD), 1.0, 6.0, ((0, 4), (1, 8))),
        "neighbours": draw_neighbours(jax.random.fold_in(key_of[7], 71), 0),
        "counts": draw_counts(jax.random.fold_in(key_of[7], 71), 0),
    }


def block_backward(query_head, key_head, value_head, grad_head, links, tallies):
    score_scale = HDIM ** -0.5
    query_blocks = query_head.reshape(NQB, BLK, HDIM).astype(jnp.float32)
    key_near = key_head.reshape(NQB, BLK, HDIM)[links].reshape(NQB, MAXNB * BLK, HDIM).astype(jnp.float32)
    value_near = value_head.reshape(NQB, BLK, HDIM)[links].reshape(NQB, MAXNB * BLK, HDIM).astype(jnp.float32)
    grad_blocks = grad_head.reshape(NQB, BLK, HDIM).astype(jnp.float32)
    live_slot = jnp.arange(MAXNB)[None, :] < tallies[:, None]
    live_keys = jnp.repeat(live_slot, BLK, axis=1)[:, None, :]
    scores = jnp.einsum("qtd,qkd->qtk", query_blocks, key_near) * score_scale
    scores = jnp.where(live_keys, scores, -jnp.inf)
    top_score = jnp.max(scores, axis=-1, keepdims=True)
    weights = jnp.exp(scores - top_score)
    probs = weights / jnp.sum(weights, axis=-1, keepdims=True)
    probs_low = lax.optimization_barrier(probs.astype(jnp.bfloat16)).astype(jnp.float32)
    value_part = jnp.einsum("qtk,qtd->qkd", probs_low, grad_blocks)
    prob_grad = jnp.einsum("qtd,qkd->qtk", grad_blocks, value_near)
    row_dot = jnp.sum(probs * prob_grad, axis=-1, keepdims=True)
    score_grad = lax.optimization_barrier((probs * (prob_grad - row_dot) * score_scale).astype(jnp.bfloat16)).astype(jnp.float32)
    query_part = jnp.einsum("qtk,qkd->qtd", score_grad, key_near)
    key_part = jnp.einsum("qtk,qtd->qkd", score_grad, query_blocks)
    flat_links = links.reshape(-1)
    key_sum = jnp.zeros((NQB, BLK, HDIM), jnp.float32).at[flat_links].add(key_part.reshape(NQB * MAXNB, BLK, HDIM))
    value_sum = jnp.zeros((NQB, BLK, HDIM), jnp.float32).at[flat_links].add(value_part.reshape(NQB * MAXNB, BLK, HDIM))
    return query_part.reshape(SNAP_TOK, HDIM), key_sum.reshape(SNAP_TOK, HDIM), value_sum.reshape(SNAP_TOK, HDIM)


def split_heads(array):
    return array.reshape(SNAP_TOK, H, HDIM).transpose(1, 0, 2)


def join_heads(array):
    return array.transpose(1, 0, 2).reshape(SNAP_TOK, HD).astype(jnp.bfloat16)


def snapshot_backward(snap_items):
    query_snap, key_snap, value_snap, grad_snap, links, tallies = snap_items

    def one_head(head_items):
        return block_backward(head_items[0], head_items[1], head_items[2], head_items[3], links, tallies)

    results = lax.map(one_head, (split_heads(query_snap), split_heads(key_snap), split_heads(value_snap), split_heads(grad_snap)))
    return join_heads(results[0]), join_heads(results[1]), join_heads(results[2])


def reference(layer_input, query_rows, key_rows, value_rows, out_grad, neighbours, counts):
    query_grad, key_grad, value_grad = lax.map(snapshot_backward, (query_rows, key_rows, value_rows, out_grad, neighbours, counts))
    pieces = []
    for grads in (query_grad, key_grad, value_grad):
        total = jnp.zeros((D, HD), jnp.float32)
        for snap in range(SNAPS):
            partial_sum = jnp.dot(layer_input[snap].T, grads[snap], preferred_element_type=jnp.float32)
            total = total + lax.optimization_barrier(partial_sum.astype(jnp.bfloat16)).astype(jnp.float32)
        pieces.append(total)
    weight_grad = jnp.stack(pieces, axis=0) * (1.0 / (TOKENS ** 0.5))
    return query_grad, key_grad, value_grad, weight_grad
```

```python
import math

import jax
import jax.numpy as jnp
from jax import lax
from jax.experimental import pallas as pl
from jax.experimental.pallas import tpu as pltpu
from jax.sharding import PartitionSpec as P

HDIM = 128
BLK = 128
MIB = 1 << 20
BF = jnp.bfloat16
F32 = jnp.float32


def pack_rows(arrays, parts, chunks):
    tokens, width = arrays[0].shape
    each = width // parts
    cut = each // chunks

    def kernel(*refs):
        ins, outs = refs[: len(arrays)], refs[len(arrays) :]
        for i, ref in enumerate(ins):
            for c, out in enumerate(outs):
                out[0, i] = ref[:, c * cut : (c + 1) * cut]

    return pl.pallas_call(
        kernel,
        grid=(parts,),
        in_specs=[pl.BlockSpec((tokens, each), lambda s: (0, s))] * len(arrays),
        out_specs=[pl.BlockSpec((1, len(arrays), tokens, cut), lambda s: (s, 0, 0, 0))] * chunks,
        out_shape=[jax.ShapeDtypeStruct((parts, len(arrays), tokens, cut), BF)] * chunks,
        name="pack_rows",
    )(*arrays)


def unpack_rows(chunked):
    parts, kinds, tokens, cut = chunked[0].shape
    chunks = len(chunked)

    def kernel(*refs):
        ins, outs = refs[:chunks], refs[chunks:]
        for i, out in enumerate(outs):
            for c, ref in enumerate(ins):
                out[:, c * cut : (c + 1) * cut] = ref[0, i]

    return pl.pallas_call(
        kernel,
        grid=(parts,),
        in_specs=[pl.BlockSpec((1, kinds, tokens, cut), lambda s: (s, 0, 0, 0))] * chunks,
        out_specs=[pl.BlockSpec((tokens, chunks * cut), lambda s: (0, s))] * kinds,
        out_shape=[jax.ShapeDtypeStruct((tokens, parts * chunks * cut), BF)] * kinds,
        name="unpack_rows",
    )(*chunked)


def turn(array):
    tokens, width = array.shape
    step = 512

    def kernel(ref, out):
        out[...] = ref[...].T

    return pl.pallas_call(
        kernel,
        grid=(width // step,),
        in_specs=[pl.BlockSpec((tokens, step), lambda i: (0, i))],
        out_specs=pl.BlockSpec((step, tokens), lambda i: (i, 0)),
        out_shape=jax.ShapeDtypeStruct((width, tokens), BF),
        name="turn_layer_input",
    )(array)


def attention(items, bias):
    blocks, _, _, width = items.shape
    heads = width // HDIM
    tokens = blocks * BLK
    pair = 2 * BLK
    factor = HDIM ** (-0.5)
    nt = (((1,), (1,)), ((), ()))

    def kernel(items_ref, bias_ref, out_ref, key_sum, value_sum):
        for h in range(heads):
            cols = slice(h * HDIM, (h + 1) * HDIM)
            keys = items_ref[:, 1, :, cols].reshape(tokens, HDIM)
            values = items_ref[:, 2, :, cols].reshape(tokens, HDIM)
            keys_t = keys.T
            key_sum[...] = jnp.zeros_like(key_sum)
            value_sum[...] = jnp.zeros_like(value_sum)

            def step(n, _):
                query = items_ref[pl.ds(2 * n, 2), 0, :, cols].reshape(pair, HDIM)
                grad = items_ref[pl.ds(2 * n, 2), 3, :, cols].reshape(pair, HDIM)
                scores = lax.dot_general(keys, query, nt, preferred_element_type=F32)
                near = bias_ref[n]
                scores = (
                    scores.reshape(blocks, BLK, pair) * (factor * math.log2(math.e)) + near[:, None, :]
                ).reshape(tokens, pair)
                top = jnp.max(scores, axis=0, keepdims=True)
                weights = jnp.exp2(scores - top)
                prob_grad = lax.dot_general(values, grad, nt, preferred_element_type=F32)
                inverse = 1.0 / jnp.sum(weights, axis=0, keepdims=True)
                row_dot = jnp.sum(weights * prob_grad, axis=0, keepdims=True) * inverse
                probs = weights * inverse
                probs_low = probs.astype(BF)
                score_grad = (probs * (prob_grad - row_dot)).astype(BF)
                value_sum[...] += jnp.dot(probs_low, grad, preferred_element_type=F32)
                key_sum[...] += jnp.dot(score_grad, query, preferred_element_type=F32)
                query_grad_t = jnp.dot(keys_t, score_grad, preferred_element_type=F32) * factor
                out_ref[pl.ds(2 * n, 2), 0, :, cols] = query_grad_t.T.astype(BF).reshape(2, BLK, HDIM)
                return 0

            lax.fori_loop(0, blocks // 2, step, 0)
            out_ref[:, 1, :, cols] = (key_sum[...] * factor).astype(BF).reshape(blocks, BLK, HDIM)
            out_ref[:, 2, :, cols] = value_sum[...].astype(BF).reshape(blocks, BLK, HDIM)

    return pl.pallas_call(
        kernel,
        in_specs=[pl.BlockSpec(memory_space=pltpu.VMEM)] * 2,
        out_specs=pl.BlockSpec(memory_space=pltpu.VMEM),
        out_shape=jax.ShapeDtypeStruct((blocks, 3, BLK, width), BF),
        scratch_shapes=[pltpu.VMEM((tokens, HDIM), F32), pltpu.VMEM((tokens, HDIM), F32)],
        compiler_params=pltpu.CompilerParams(vmem_limit_bytes=40 * MIB),
        cost_estimate=pl.CostEstimate(
            flops=20 * heads * tokens * tokens * HDIM,
            bytes_accessed=14 * tokens * width,
            transcendentals=heads * tokens * tokens,
        ),
        name="attention_backward",
    )(items, bias)


def weight_products(turned, grads, norm):
    blocks, snaps, rows, _ = turned.shape
    chunks = len(grads[0])
    cut = grads[0][0].shape[-1]
    flat = [grads[k][c] for k in range(snaps) for c in range(chunks)]
    group = 4
    row_step = rows // 2

    def kernel(*refs):
        turned_ref, grad_refs, out_ref = refs[0], refs[1:-1], refs[-1]
        at = pl.program_id(1)

        @pl.when(at == 0)
        def _():
            out_ref[...] = jnp.zeros_like(out_ref)

        for k in range(snaps):
            left = jnp.concatenate([turned_ref[b, k] for b in range(group)], axis=1)
            for c in range(chunks):
                ref = grad_refs[k * chunks + c]
                for kind in range(3):
                    right = ref[:, kind].reshape(group * BLK, cut)
                    out_ref[kind, :, c * cut : (c + 1) * cut] += jnp.dot(
                        left, right, preferred_element_type=F32
                    )

        @pl.when(at == pl.num_programs(1) - 1)
        def _():
            out_ref[...] = out_ref[...] * norm

    return pl.pallas_call(
        kernel,
        grid=(2, blocks // group),
        in_specs=[pl.BlockSpec((group, snaps, row_step, BLK), lambda r, b: (b, 0, r, 0))]
        + [pl.BlockSpec((group, 3, BLK, cut), lambda r, b: (b, 0, 0, 0))] * len(flat),
        out_specs=pl.BlockSpec((3, row_step, chunks * cut), lambda r, b: (0, r, 0)),
        out_shape=jax.ShapeDtypeStruct((3, rows, chunks * cut), F32),
        compiler_params=pltpu.CompilerParams(vmem_limit_bytes=56 * MIB),
        cost_estimate=pl.CostEstimate(
            flops=6 * blocks * BLK * snaps * rows * chunks * cut,
            bytes_accessed=2 * blocks * snaps * BLK * (rows + 3 * chunks * cut) + 12 * rows * chunks * cut,
            transcendentals=0,
        ),
        name="weight_products",
    )(turned, *flat)


def local(layer_input, query_rows, key_rows, value_rows, out_grad, neighbours, counts):
    seq_count = lax.axis_size("seq")
    dp_count = lax.axis_size("dp")
    here = lax.axis_index("dp")
    width = query_rows.shape[2]
    heads_here = width // seq_count // HDIM
    blocks = neighbours.shape[1]
    chunks = 2 if heads_here % 2 == 0 else 1
    rows_here = layer_input.shape[2] // dp_count
    y_count = dp_count // 2

    def peer(p, j, e):
        return ((p // 2 + j) % y_count) * 2 + ((p % 2) ^ e)

    peers = [(j, e) for j in range(y_count) for e in range(2)]

    def dp_move(array, j, e):
        return lax.ppermute(array, "dp", [(peer(p, j, e), p) for p in range(dp_count)])

    packed = pack_rows([query_rows[0], key_rows[0], value_rows[0], out_grad[0]], seq_count, chunks)

    turned = turn(layer_input[0])
    slabs = []
    for j, e in peers:
        to = peer(here, (y_count - j) % y_count, e)
        slab = lax.dynamic_slice_in_dim(turned, to * rows_here, rows_here, 0)
        slabs.append(slab if (j, e) == (0, 0) else dp_move(slab, j, e))
    turned_all = lax.all_gather(jnp.stack(slabs), "seq", axis=0, tiled=False)

    live = jnp.arange(neighbours.shape[2])[None, :] < counts[0][:, None]
    hit = (neighbours[0][:, :, None] == jnp.arange(blocks)[None, None, :]) & live[:, :, None]
    near = jnp.where(jnp.any(hit, axis=1), 0.0, -jnp.inf).astype(F32)
    bias = jnp.repeat(near.reshape(blocks // 2, 2, blocks).transpose(0, 2, 1), BLK, axis=2)

    grads = [[None] * chunks for _ in peers]
    back = []
    for c in range(chunks):
        items = lax.all_to_all(packed[c], "seq", 0, 0, tiled=True)
        out = attention(items, bias)
        back.append(lax.all_to_all(out, "seq", 0, 0, tiled=True))
        for n, (j, e) in enumerate(peers):
            if e == 0:
                grads[n][c] = out if j == 0 else dp_move(out, j, 0)
        for n, (j, e) in enumerate(peers):
            if e == 1:
                grads[n][c] = dp_move(grads[n - 1][c], 0, 1)
    norm = 1.0 / math.sqrt(neighbours.shape[1] * BLK * dp_count)
    weight_grad = weight_products(turned_all, grads, norm)
    query_grad, key_grad, value_grad = unpack_rows(back)
    return query_grad[None], key_grad[None], value_grad[None], weight_grad


def solution(mesh):
    placed = (P("dp", "seq", None),) * 5 + (P("dp", None, None), P("dp", None))
    return jax.shard_map(
        local,
        mesh=mesh,
        in_specs=placed,
        out_specs=(P("dp", "seq", None),) * 3 + (P(None, "dp", "seq"),),
        check_vma=False,
    )
```

```python
import math

import jax
import jax.numpy as jnp
from jax import lax
from jax.experimental import pallas as pl
from jax.experimental.pallas import tpu as pltpu
from jax.sharding import PartitionSpec as P

HDIM = 128
BLK = 128
MIB = 1 << 20
BF = jnp.bfloat16
F32 = jnp.float32


def move_pieces(pairs, buffer, sems):
    ins = [pltpu.make_async_copy(a, buffer.at[n], sems.at[0, n]) for n, (a, _) in enumerate(pairs)]
    outs = [pltpu.make_async_copy(buffer.at[n], b, sems.at[1, n]) for n, (_, b) in enumerate(pairs)]
    for copy in ins:
        copy.start()
    for copy, then in zip(ins, outs):
        copy.wait()
        then.start()
    for copy in outs:
        copy.wait()


def pack_rows(arrays, parts, chunk, chunks, after=()):
    tokens, width = arrays[0].shape
    cut = width // parts // chunks
    kinds = len(arrays)

    def kernel(*refs):
        ins, (out, buffer, sems) = refs[:kinds], refs[-3:]
        pairs = [
            (ins[i].at[:, pl.ds((s * chunks + chunk) * cut, cut)], out.at[s, i])
            for s in range(parts)
            for i in range(kinds)
        ]
        move_pieces(pairs, buffer, sems)

    return pl.pallas_call(
        kernel,
        in_specs=[pl.BlockSpec(memory_space=pl.ANY)] * (kinds + len(after)),
        out_specs=pl.BlockSpec(memory_space=pl.ANY),
        out_shape=jax.ShapeDtypeStruct((parts, kinds, tokens, cut), BF),
        scratch_shapes=[
            pltpu.VMEM((parts * kinds, tokens, cut), BF),
            pltpu.SemaphoreType.DMA((2, parts * kinds)),
        ],
        cost_estimate=pl.CostEstimate(
            flops=0, bytes_accessed=4 * kinds * tokens * parts * cut, transcendentals=0
        ),
        name="pack_rows",
    )(*arrays, *after)


def unpack_rows(packed, chunk, chunks, before, after=()):
    parts, kinds, tokens, cut = packed.shape
    before = before or []

    def kernel(*refs):
        ref, outs, (buffer, sems) = refs[0], refs[-2 - kinds : -2], refs[-2:]
        pairs = [
            (ref.at[s, i], outs[i].at[:, pl.ds((s * chunks + chunk) * cut, cut)])
            for s in range(parts)
            for i in range(kinds)
        ]
        move_pieces(pairs, buffer, sems)

    return pl.pallas_call(
        kernel,
        in_specs=[pl.BlockSpec(memory_space=pl.ANY)] * (1 + len(before) + len(after)),
        out_specs=[pl.BlockSpec(memory_space=pl.ANY)] * kinds,
        out_shape=[jax.ShapeDtypeStruct((tokens, parts * chunks * cut), BF)] * kinds,
        scratch_shapes=[
            pltpu.VMEM((parts * kinds, tokens, cut), BF),
            pltpu.SemaphoreType.DMA((2, parts * kinds)),
        ],
        input_output_aliases={1 + i: i for i in range(len(before))},
        cost_estimate=pl.CostEstimate(
            flops=0, bytes_accessed=4 * kinds * tokens * parts * cut, transcendentals=0
        ),
        name="unpack_rows",
    )(packed, *before, *after)


def hold(array, after):
    def kernel(*refs):
        pass

    return pl.pallas_call(
        kernel,
        in_specs=[pl.BlockSpec(memory_space=pl.ANY)] * (1 + len(after)),
        out_specs=pl.BlockSpec(memory_space=pl.ANY),
        out_shape=jax.ShapeDtypeStruct(array.shape, array.dtype),
        input_output_aliases={0: 0},
        name="hold",
    )(array, *after)


def turn(array, after=()):
    tokens, width = array.shape
    step = width // 2

    def kernel(*refs):
        refs[-1][...] = refs[0][...].T

    return pl.pallas_call(
        kernel,
        grid=(width // step,),
        in_specs=[pl.BlockSpec((tokens, step), lambda i: (0, i))]
        + [pl.BlockSpec(memory_space=pl.ANY)] * len(after),
        out_specs=pl.BlockSpec((step, tokens), lambda i: (i, 0)),
        out_shape=jax.ShapeDtypeStruct((width, tokens), BF),
        name="turn_layer_input",
    )(array, *after)


def attention(items, bias, after=()):
    blocks, _, _, width = items.shape
    heads = width // HDIM
    tokens = blocks * BLK
    pair = 2 * BLK
    factor = HDIM ** (-0.5)
    nt = (((1,), (1,)), ((), ()))

    def kernel(*refs):
        items_ref, bias_ref = refs[:2]
        out_ref, key_sum, value_sum = refs[-3:]
        for h in range(heads):
            cols = slice(h * HDIM, (h + 1) * HDIM)
            keys = items_ref[:, 1, :, cols].reshape(tokens, HDIM)
            values = items_ref[:, 2, :, cols].reshape(tokens, HDIM)
            keys_t = keys.T
            key_sum[...] = jnp.zeros_like(key_sum)
            value_sum[...] = jnp.zeros_like(value_sum)

            def step(n, _):
                query = items_ref[pl.ds(2 * n, 2), 0, :, cols].reshape(pair, HDIM)
                grad = items_ref[pl.ds(2 * n, 2), 3, :, cols].reshape(pair, HDIM)
                scores = lax.dot_general(keys, query, nt, preferred_element_type=F32)
                near = bias_ref[n]
                scores = (
                    scores.reshape(blocks, BLK, pair) * (factor * math.log2(math.e)) + near[:, None, :]
                ).reshape(tokens, pair)
                top = jnp.max(scores, axis=0, keepdims=True)
                weights = jnp.exp2(scores - top)
                prob_grad = lax.dot_general(values, grad, nt, preferred_element_type=F32)
                inverse = 1.0 / jnp.sum(weights, axis=0, keepdims=True)
                row_dot = jnp.sum(weights * prob_grad, axis=0, keepdims=True) * inverse
                probs = weights * inverse
                probs_low = probs.astype(BF)
                score_grad = (probs * (prob_grad - row_dot)).astype(BF)
                value_sum[...] += jnp.dot(probs_low, grad, preferred_element_type=F32)
                key_sum[...] += jnp.dot(score_grad, query, preferred_element_type=F32)
                query_grad_t = jnp.dot(keys_t, score_grad, preferred_element_type=F32) * factor
                out_ref[pl.ds(2 * n, 2), 0, :, cols] = query_grad_t.T.astype(BF).reshape(2, BLK, HDIM)
                return 0

            lax.fori_loop(0, blocks // 2, step, 0)
            out_ref[:, 1, :, cols] = (key_sum[...] * factor).astype(BF).reshape(blocks, BLK, HDIM)
            out_ref[:, 2, :, cols] = value_sum[...].astype(BF).reshape(blocks, BLK, HDIM)

    return pl.pallas_call(
        kernel,
        in_specs=[pl.BlockSpec(memory_space=pltpu.VMEM)] * 2 + [pl.BlockSpec(memory_space=pl.ANY)] * len(after),
        out_specs=pl.BlockSpec(memory_space=pltpu.VMEM),
        out_shape=jax.ShapeDtypeStruct((blocks, 3, BLK, width), BF),
        scratch_shapes=[pltpu.VMEM((tokens, HDIM), F32), pltpu.VMEM((tokens, HDIM), F32)],
        compiler_params=pltpu.CompilerParams(vmem_limit_bytes=40 * MIB),
        cost_estimate=pl.CostEstimate(
            flops=20 * heads * tokens * tokens * HDIM,
            bytes_accessed=14 * tokens * width,
            transcendentals=heads * tokens * tokens,
        ),
        name="attention_backward",
    )(items, bias, *after)


def weight_products(units, places, grads, chunk, chunks, norm, before):
    blocks = len(units)
    snaps, rows, _ = units[0].shape
    cut = grads[0].shape[-1]
    group = 4
    steps = 4
    row_step = rows // steps
    before = [] if before is None else [before]

    def kernel(*refs):
        places_ref, unit_refs, grad_refs = refs[0], refs[1 : 1 + blocks], refs[1 + blocks : 1 + blocks + snaps]
        out_ref = refs[-1]
        for start in range(0, blocks, group):
            for k in range(snaps):
                left = jnp.concatenate([unit_refs[start + u][k] for u in range(group)], axis=1)
                for kind in range(3):
                    right = jnp.concatenate(
                        [grad_refs[k][places_ref[start + u], kind] for u in range(group)], axis=0
                    )
                    part = jnp.dot(left, right, preferred_element_type=F32)
                    if start == 0 and k == 0:
                        out_ref[kind] = part
                    elif start + group == blocks and k == snaps - 1:
                        out_ref[kind] = (out_ref[kind] + part) * norm
                    else:
                        out_ref[kind] += part

    return pl.pallas_call(
        kernel,
        grid_spec=pltpu.PrefetchScalarGridSpec(
            num_scalar_prefetch=1,
            grid=(steps,),
            in_specs=[pl.BlockSpec((snaps, row_step, BLK), lambda r, _: (0, r, 0))] * blocks
            + [pl.BlockSpec((blocks, 3, BLK, cut), lambda r, _: (0, 0, 0, 0))] * snaps
            + [pl.BlockSpec(memory_space=pl.ANY)] * len(before),
            out_specs=pl.BlockSpec((3, row_step, cut), lambda r, _: (0, r, chunk)),
        ),
        out_shape=jax.ShapeDtypeStruct((3, rows, chunks * cut), F32),
        input_output_aliases={1 + blocks + snaps: 0} if before else {},
        compiler_params=pltpu.CompilerParams(vmem_limit_bytes=56 * MIB),
        cost_estimate=pl.CostEstimate(
            flops=6 * blocks * BLK * snaps * rows * cut,
            bytes_accessed=2 * blocks * snaps * BLK * (rows + 3 * cut) + 12 * rows * cut,
            transcendentals=0,
        ),
        name="weight_products",
    )(places, *units, *grads, *before)


def seq_swap(array, bit):
    return lax.ppermute(array, "seq", [(i, i ^ bit) for i in range(lax.axis_size("seq"))])


def local(layer_input, query_rows, key_rows, value_rows, out_grad, neighbours, counts):
    seq_count = lax.axis_size("seq")
    dp_count = lax.axis_size("dp")
    here = lax.axis_index("dp")
    width = query_rows.shape[2]
    heads_here = width // seq_count // HDIM
    blocks = neighbours.shape[1]
    chunks = 2 if heads_here % 2 == 0 else 1
    rows_here = layer_input.shape[2] // dp_count
    y_count = dp_count // 2

    def peer(p, j, e):
        return ((p // 2 + j) % y_count) * 2 + ((p % 2) ^ e)

    peers = [(j, e) for j in range(y_count) for e in range(2)]

    def dp_move(array, j, e):
        return lax.ppermute(array, "dp", [(peer(p, j, e), p) for p in range(dp_count)])

    rows_in = [query_rows[0], key_rows[0], value_rows[0], out_grad[0]]
    live = jnp.arange(neighbours.shape[2])[None, :] < counts[0][:, None]
    hit = (neighbours[0][:, :, None] == jnp.arange(blocks)[None, None, :]) & live[:, :, None]
    near = jnp.where(jnp.any(hit, axis=1), 0.0, -jnp.inf).astype(F32)
    bias = jnp.repeat(near.reshape(blocks // 2, 2, blocks).transpose(0, 2, 1), BLK, axis=2)

    packed = [pack_rows(rows_in, seq_count, 0, chunks)]
    items = [lax.all_to_all(packed[0], "seq", 0, 0, tiled=True)]

    turned = turn(layer_input[0], packed)
    slabs = []
    for j, e in peers:
        to = peer(here, (y_count - j) % y_count, e)
        slab = lax.dynamic_slice_in_dim(turned, to * rows_here, rows_here, 0)
        slabs.append(slab if (j, e) == (0, 0) else dp_move(slab, j, e))
    packed += [pack_rows(rows_in, seq_count, c, chunks, [turned]) for c in range(1, chunks)]
    own = jnp.stack(slabs)
    at = lax.axis_index("seq")
    ready, behind = [[] for _ in range(chunks)], [[], []]
    if seq_count == 8:
        beside, far, own_x = seq_swap(own, 2), seq_swap(own, 4), seq_swap(own, 1)
        beside_x = seq_swap(beside, 1)
        for c in range(1, chunks):
            packed[c] = hold(packed[c], [beside, far, own_x, beside_x])
        ready[0] = packed[1:2]
        far_beside, far_x = seq_swap(far, 2), seq_swap(far, 1)
        far_beside_x = seq_swap(far_beside, 1)
        behind = [[far_beside, far_x], [far_beside_x]]
        units = [own, beside, far, far_beside, own_x, beside_x, far_x, far_beside_x]
        places = jnp.stack([at ^ bits for bits in (0, 2, 4, 6, 1, 3, 5, 7)]).astype(jnp.int32)
    else:
        every = lax.all_gather(own, "seq", axis=0, tiled=False)
        units, places = [every[i] for i in range(seq_count)], jnp.arange(seq_count, dtype=jnp.int32)
    items += [lax.all_to_all(a, "seq", 0, 0, tiled=True) for a in packed[1:]]

    norm = 1.0 / math.sqrt(neighbours.shape[1] * BLK * dp_count)
    weight_grad, done = None, None
    for c in range(chunks):
        out = attention(items[c], bias, ready[c])
        over_y = [out] + [dp_move(out, j, 0) for j in range(1, y_count)]
        grads = [a for there in over_y for a in (there, dp_move(there, 0, 1))]
        late = behind[c] + (over_y[1:] if c == 0 else [])
        back = hold(out, late) if late and chunks == 2 else out
        back = lax.all_to_all(back, "seq", 0, 0, tiled=True)
        weight_grad = weight_products(units, places, grads, c, chunks, norm, weight_grad)
        done = unpack_rows(back, c, chunks, done, [weight_grad] if c == chunks - 1 else [])
    query_grad, key_grad, value_grad = done
    return query_grad[None], key_grad[None], value_grad[None], weight_grad


def solution(mesh):
    placed = (P("dp", "seq", None),) * 5 + (P("dp", None, None), P("dp", None))
    return jax.shard_map(
        local,
        mesh=mesh,
        in_specs=placed,
        out_specs=(P("dp", "seq", None),) * 3 + (P(None, "dp", "seq"),),
        check_vma=False,
    )
```

```python
import math

import jax
import jax.numpy as jnp
from jax import lax
from jax.experimental import pallas as pl
from jax.experimental.pallas import tpu as pltpu
from jax.sharding import PartitionSpec as P

HDIM = 128
BLK = 128
MIB = 1 << 20
BF = jnp.bfloat16
F32 = jnp.float32
HOLD_1 = [(2, 0), (2, 1), (4, 0), (4, 1), (1, 0), (1, 1), (3, 0), (3, 1)]
HOLD_2 = [(6, 0), (5, 0), (5, 1)]
LATE = [(7, 1)]
HOLD_3 = [(6, 1), (7, 0)]


def move_pieces(pairs, buffer, sems):
    ins = [pltpu.make_async_copy(a, buffer.at[n], sems.at[0, n]) for n, (a, _) in enumerate(pairs)]
    outs = [pltpu.make_async_copy(buffer.at[n], b, sems.at[1, n]) for n, (_, b) in enumerate(pairs)]
    for copy in ins:
        copy.start()
    for copy, then in zip(ins, outs):
        copy.wait()
        then.start()
    for copy in outs:
        copy.wait()


def pack_rows(arrays, parts, chunk, chunks, after=()):
    tokens, width = arrays[0].shape
    cut = width // parts // chunks
    kinds = len(arrays)

    def kernel(*refs):
        ins, (out, buffer, sems) = refs[:kinds], refs[-3:]
        pairs = [
            (ins[i].at[:, pl.ds((s * chunks + chunk) * cut, cut)], out.at[s, i])
            for s in range(parts)
            for i in range(kinds)
        ]
        move_pieces(pairs, buffer, sems)

    return pl.pallas_call(
        kernel,
        in_specs=[pl.BlockSpec(memory_space=pl.ANY)] * (kinds + len(after)),
        out_specs=pl.BlockSpec(memory_space=pl.ANY),
        out_shape=jax.ShapeDtypeStruct((parts, kinds, tokens, cut), BF),
        scratch_shapes=[
            pltpu.VMEM((parts * kinds, tokens, cut), BF),
            pltpu.SemaphoreType.DMA((2, parts * kinds)),
        ],
        cost_estimate=pl.CostEstimate(
            flops=0, bytes_accessed=4 * kinds * tokens * parts * cut, transcendentals=0
        ),
        name="pack_rows",
    )(*arrays, *after)


def unpack_rows(packed, chunk, chunks, before, after=()):
    parts, kinds, tokens, cut = packed.shape
    before = before or []

    def kernel(*refs):
        ref, outs, (buffer, sems) = refs[0], refs[-2 - kinds : -2], refs[-2:]
        pairs = [
            (ref.at[s, i], outs[i].at[:, pl.ds((s * chunks + chunk) * cut, cut)])
            for s in range(parts)
            for i in range(kinds)
        ]
        move_pieces(pairs, buffer, sems)

    return pl.pallas_call(
        kernel,
        in_specs=[pl.BlockSpec(memory_space=pl.ANY)] * (1 + len(before) + len(after)),
        out_specs=[pl.BlockSpec(memory_space=pl.ANY)] * kinds,
        out_shape=[jax.ShapeDtypeStruct((tokens, parts * chunks * cut), BF)] * kinds,
        scratch_shapes=[
            pltpu.VMEM((parts * kinds, tokens, cut), BF),
            pltpu.SemaphoreType.DMA((2, parts * kinds)),
        ],
        input_output_aliases={1 + i: i for i in range(len(before))},
        cost_estimate=pl.CostEstimate(
            flops=0, bytes_accessed=4 * kinds * tokens * parts * cut, transcendentals=0
        ),
        name="unpack_rows",
    )(packed, *before, *after)


def hold(array, after):
    def kernel(*refs):
        pass

    return pl.pallas_call(
        kernel,
        in_specs=[pl.BlockSpec(memory_space=pl.ANY)] * (1 + len(after)),
        out_specs=pl.BlockSpec(memory_space=pl.ANY),
        out_shape=jax.ShapeDtypeStruct(array.shape, array.dtype),
        input_output_aliases={0: 0},
        name="hold",
    )(array, *after)


def turn(array, after=()):
    tokens, width = array.shape
    step = width // 2

    def kernel(*refs):
        refs[-1][...] = refs[0][...].T

    return pl.pallas_call(
        kernel,
        grid=(width // step,),
        in_specs=[pl.BlockSpec((tokens, step), lambda i: (0, i))]
        + [pl.BlockSpec(memory_space=pl.ANY)] * len(after),
        out_specs=pl.BlockSpec((step, tokens), lambda i: (i, 0)),
        out_shape=jax.ShapeDtypeStruct((width, tokens), BF),
        name="turn_layer_input",
    )(array, *after)


def attention(items, bias, after=()):
    blocks, _, _, width = items.shape
    heads = width // HDIM
    tokens = blocks * BLK
    pair = 2 * BLK
    factor = HDIM ** (-0.5)
    nt = (((1,), (1,)), ((), ()))

    def kernel(*refs):
        items_ref, bias_ref = refs[:2]
        out_ref, key_sum, value_sum = refs[-3:]
        for h in range(heads):
            cols = slice(h * HDIM, (h + 1) * HDIM)
            keys = items_ref[:, 1, :, cols].reshape(tokens, HDIM)
            values = items_ref[:, 2, :, cols].reshape(tokens, HDIM)
            keys_t = keys.T
            key_sum[...] = jnp.zeros_like(key_sum)
            value_sum[...] = jnp.zeros_like(value_sum)

            def step(n, _):
                query = items_ref[pl.ds(2 * n, 2), 0, :, cols].reshape(pair, HDIM)
                grad = items_ref[pl.ds(2 * n, 2), 3, :, cols].reshape(pair, HDIM)
                scores = lax.dot_general(keys, query, nt, preferred_element_type=F32)
                near = bias_ref[n]
                scores = (
                    scores.reshape(blocks, BLK, pair) * (factor * math.log2(math.e)) + near[:, None, :]
                ).reshape(tokens, pair)
                top = jnp.max(scores, axis=0, keepdims=True)
                weights = jnp.exp2(scores - top)
                prob_grad = lax.dot_general(values, grad, nt, preferred_element_type=F32)
                inverse = 1.0 / jnp.sum(weights, axis=0, keepdims=True)
                row_dot = jnp.sum(weights * prob_grad, axis=0, keepdims=True) * inverse
                probs = weights * inverse
                probs_low = probs.astype(BF)
                score_grad = (probs * (prob_grad - row_dot)).astype(BF)
                value_sum[...] += jnp.dot(probs_low, grad, preferred_element_type=F32)
                key_sum[...] += jnp.dot(score_grad, query, preferred_element_type=F32)
                query_grad_t = jnp.dot(keys_t, score_grad, preferred_element_type=F32) * factor
                out_ref[pl.ds(2 * n, 2), 0, :, cols] = query_grad_t.T.astype(BF).reshape(2, BLK, HDIM)
                return 0

            lax.fori_loop(0, blocks // 2, step, 0)
            out_ref[:, 1, :, cols] = (key_sum[...] * factor).astype(BF).reshape(blocks, BLK, HDIM)
            out_ref[:, 2, :, cols] = value_sum[...].astype(BF).reshape(blocks, BLK, HDIM)

    return pl.pallas_call(
        kernel,
        in_specs=[pl.BlockSpec(memory_space=pltpu.VMEM)] * 2 + [pl.BlockSpec(memory_space=pl.ANY)] * len(after),
        out_specs=pl.BlockSpec(memory_space=pltpu.VMEM),
        out_shape=jax.ShapeDtypeStruct((blocks, 3, BLK, width), BF),
        scratch_shapes=[pltpu.VMEM((tokens, HDIM), F32), pltpu.VMEM((tokens, HDIM), F32)],
        compiler_params=pltpu.CompilerParams(vmem_limit_bytes=40 * MIB),
        cost_estimate=pl.CostEstimate(
            flops=20 * heads * tokens * tokens * HDIM,
            bytes_accessed=14 * tokens * width,
            transcendentals=heads * tokens * tokens,
        ),
        name="attention_backward",
    )(items, bias, *after)


def weight_products(units, places, grads, chunk, chunks, norm, before):
    blocks, snaps = len(units), len(grads)
    rows = units[0][0][0].shape[1]
    cut = grads[0].shape[-1]
    group = 4
    steps = 4
    row_step = rows // steps
    before = [] if before is None else [before]
    flat = [piece for unit in units for piece, _ in unit]
    spots, at = [], 0
    for unit in units:
        spot = {}
        for piece, snap in unit:
            spot.update({snap + i: (at, i) for i in range(piece.shape[0])})
            at += 1
        spots.append(spot)

    def kernel(*refs):
        places_ref, unit_refs = refs[0], refs[1 : 1 + len(flat)]
        grad_refs, out_ref = refs[1 + len(flat) : 1 + len(flat) + snaps], refs[-1]
        for start in range(0, blocks, group):
            for k in range(snaps):
                here = [u for u in range(start, min(start + group, blocks)) if k in spots[u]]
                near = [spots[u][k] for u in here]
                left = jnp.concatenate([unit_refs[n][i] for n, i in near], axis=1)
                for kind in range(3):
                    right = jnp.concatenate([grad_refs[k][places_ref[u], kind] for u in here], axis=0)
                    part = jnp.dot(left, right, preferred_element_type=F32)
                    if start > 0 or k > 0:
                        part = out_ref[kind] + part
                    out_ref[kind] = part * norm if start + group >= blocks and k == snaps - 1 else part

    return pl.pallas_call(
        kernel,
        grid_spec=pltpu.PrefetchScalarGridSpec(
            num_scalar_prefetch=1,
            grid=(steps,),
            in_specs=[pl.BlockSpec((a.shape[0], row_step, BLK), lambda r, _: (0, r, 0)) for a in flat]
            + [pl.BlockSpec((blocks, 3, BLK, cut), lambda r, _: (0, 0, 0, 0))] * snaps
            + [pl.BlockSpec(memory_space=pl.ANY)] * len(before),
            out_specs=pl.BlockSpec((3, row_step, cut), lambda r, _: (0, r, chunk)),
        ),
        out_shape=jax.ShapeDtypeStruct((3, rows, chunks * cut), F32),
        input_output_aliases={1 + len(flat) + snaps: 0} if before else {},
        compiler_params=pltpu.CompilerParams(vmem_limit_bytes=56 * MIB),
        cost_estimate=pl.CostEstimate(
            flops=6 * blocks * BLK * snaps * rows * cut,
            bytes_accessed=2 * blocks * snaps * BLK * (rows + 3 * cut) + 12 * rows * cut,
            transcendentals=0,
        ),
        name="weight_products",
    )(places, *flat, *grads, *before)


def add_products(pieces, places, grads, norm, total):
    chunks, cut = len(grads[0]), grads[0][0].shape[-1]
    _, rows, columns = total.shape
    steps = 4
    row_step = rows // steps
    needed = [(u, n, i, snap + i) for n, (u, piece, snap) in enumerate(pieces) for i in range(piece.shape[0])]

    def kernel(*refs):
        piece_refs, grad_refs = refs[1 : 1 + len(pieces)], refs[1 + len(pieces) : -2]
        total_ref, out_ref = refs[-2:]
        left = jnp.concatenate([piece_refs[n][i] for _, n, i, _ in needed], axis=1)
        for c in range(chunks):
            for kind in range(3):
                right = jnp.concatenate([grad_refs[m * chunks + c][0, kind] for m in range(len(needed))], axis=0)
                part = jnp.dot(left, right, preferred_element_type=F32)
                cols = slice(c * cut, (c + 1) * cut)
                out_ref[kind, :, cols] = (total_ref[kind, :, cols] + part) * norm

    def block_of(u):
        return pl.BlockSpec((1, 3, BLK, cut), lambda r, places_ref: (places_ref[u], 0, 0, 0))

    whole = pl.BlockSpec((3, row_step, columns), lambda r, _: (0, r, 0))
    return pl.pallas_call(
        kernel,
        grid_spec=pltpu.PrefetchScalarGridSpec(
            num_scalar_prefetch=1,
            grid=(steps,),
            in_specs=[pl.BlockSpec((p.shape[0], row_step, BLK), lambda r, _: (0, r, 0)) for _, p, _ in pieces]
            + [block_of(u) for u, _, _, _ in needed for _ in range(chunks)]
            + [whole],
            out_specs=whole,
        ),
        out_shape=jax.ShapeDtypeStruct(total.shape, F32),
        input_output_aliases={1 + len(pieces) + len(needed) * chunks: 0},
        compiler_params=pltpu.CompilerParams(vmem_limit_bytes=32 * MIB),
        cost_estimate=pl.CostEstimate(
            flops=6 * len(needed) * BLK * rows * columns,
            bytes_accessed=24 * rows * columns,
            transcendentals=0,
        ),
        name="add_products",
    )(places, *[p for _, p, _ in pieces], *[g for _, _, _, k in needed for g in grads[k]], total)


def seq_swap(array, bit):
    return lax.ppermute(array, "seq", [(i, i ^ bit) for i in range(lax.axis_size("seq"))])


def local(layer_input, query_rows, key_rows, value_rows, out_grad, neighbours, counts):
    seq_count = lax.axis_size("seq")
    dp_count = lax.axis_size("dp")
    here = lax.axis_index("dp")
    width = query_rows.shape[2]
    heads_here = width // seq_count // HDIM
    blocks = neighbours.shape[1]
    chunks = 2 if heads_here % 2 == 0 else 1
    rows_here = layer_input.shape[2] // dp_count
    y_count = dp_count // 2

    def peer(p, j, e):
        return ((p // 2 + j) % y_count) * 2 + ((p % 2) ^ e)

    peers = [(j, e) for j in range(y_count) for e in range(2)]

    def dp_move(array, j, e):
        return lax.ppermute(array, "dp", [(peer(p, j, e), p) for p in range(dp_count)])

    rows_in = [query_rows[0], key_rows[0], value_rows[0], out_grad[0]]
    live = jnp.arange(neighbours.shape[2])[None, :] < counts[0][:, None]
    hit = (neighbours[0][:, :, None] == jnp.arange(blocks)[None, None, :]) & live[:, :, None]
    near = jnp.where(jnp.any(hit, axis=1), 0.0, -jnp.inf).astype(F32)
    bias = jnp.repeat(near.reshape(blocks // 2, 2, blocks).transpose(0, 2, 1), BLK, axis=2)

    packed = [pack_rows(rows_in, seq_count, 0, chunks)]
    items = [lax.all_to_all(packed[0], "seq", 0, 0, tiled=True)]

    turned = turn(layer_input[0], packed)
    slabs = []
    for j, e in peers:
        to = peer(here, (y_count - j) % y_count, e)
        slab = lax.dynamic_slice_in_dim(turned, to * rows_here, rows_here, 0)
        slabs.append(slab if (j, e) == (0, 0) else dp_move(slab, j, e))
    packed += [pack_rows(rows_in, seq_count, c, chunks, [turned]) for c in range(1, chunks)]
    own = [jnp.stack(slabs[: dp_count // 2]), jnp.stack(slabs[dp_count // 2 :])]
    at = lax.axis_index("seq")
    ready, behind = [[] for _ in range(chunks)], [[], []]
    if seq_count == 8:
        units = {0: own}
        for bits, source, step in ((2, 0, 2), (4, 0, 4), (6, 4, 2), (1, 0, 1), (3, 2, 1), (5, 4, 1), (7, 6, 1)):
            units[bits] = [seq_swap(a, step) for a in units[source]]
        for c in range(1, chunks):
            packed[c] = hold(packed[c], [units[n][h] for n, h in HOLD_1])
        ready[0] = packed[1:2]
        behind = [[units[n][h] for n, h in HOLD_2], [units[n][h] for n, h in HOLD_3]]
        places = jnp.stack([at ^ bits for bits in units]).astype(jnp.int32)
        late = [(list(units).index(n), units[n][h], h * (dp_count // 2)) for n, h in LATE]
        units = [
            [(a, h * (dp_count // 2)) for h, a in enumerate(halves) if (n, h) not in LATE]
            for n, halves in units.items()
        ]
    else:
        every = [lax.all_gather(half, "seq", axis=0, tiled=False) for half in own]
        units = [[(half[i], h * (dp_count // 2)) for h, half in enumerate(every)] for i in range(seq_count)]
        late = []
        places = jnp.arange(seq_count, dtype=jnp.int32)
    items += [lax.all_to_all(a, "seq", 0, 0, tiled=True) for a in packed[1:]]

    norm = 1.0 / math.sqrt(neighbours.shape[1] * BLK * dp_count)
    weight_grad, backs, every_grad = None, [], []
    for c in range(chunks):
        out = attention(items[c], bias, ready[c])
        over_y = [out] + [dp_move(out, j, 0) for j in range(1, y_count)]
        grads = [a for there in over_y for a in (there, dp_move(there, 0, 1))]
        wait = behind[c] + (over_y[1:] if c == 0 else [])
        back = hold(out, wait) if wait and chunks == 2 else out
        backs.append(lax.all_to_all(back, "seq", 0, 0, tiled=True))
        weight_grad = weight_products(units, places, grads, c, chunks, 1.0 if late else norm, weight_grad)
        every_grad.append(grads)
    if late:
        weight_grad = add_products(late, places, list(zip(*every_grad)), norm, weight_grad)
    done = None
    for c in range(chunks):
        done = unpack_rows(backs[c], c, chunks, done, [weight_grad] if c == chunks - 1 else [])
    query_grad, key_grad, value_grad = done
    return query_grad[None], key_grad[None], value_grad[None], weight_grad


def solution(mesh):
    placed = (P("dp", "seq", None),) * 5 + (P("dp", None, None), P("dp", None))
    return jax.shard_map(
        local,
        mesh=mesh,
        in_specs=placed,
        out_specs=(P("dp", "seq", None),) * 3 + (P(None, "dp", "seq"),),
        check_vma=False,
    )
```

```python
import math

import jax
import jax.numpy as jnp
from jax import lax
from jax.experimental import pallas as pl
from jax.experimental.pallas import tpu as pltpu
from jax.sharding import PartitionSpec as P

HDIM = 128
BLK = 128
MIB = 1 << 20
BF = jnp.bfloat16
F32 = jnp.float32
HOLD_1 = [(2, 0), (2, 1), (4, 0), (4, 1), (1, 0), (3, 0), (3, 1)]
HOLD_2 = [(6, 0), (5, 0), (5, 1)]
HOLD_3 = [(6, 1), (7, 0)]
LATE = [(6, 1), (7, 0), (7, 1)]
EARLY = True
HALVED = (2, 4)


def move_pieces(pairs, buffer, sems):
    ins = [pltpu.make_async_copy(a, buffer.at[n], sems.at[0, n]) for n, (a, _) in enumerate(pairs)]
    outs = [pltpu.make_async_copy(buffer.at[n], b, sems.at[1, n]) for n, (_, b) in enumerate(pairs)]
    for copy in ins:
        copy.start()
    for copy, then in zip(ins, outs):
        copy.wait()
        then.start()
    for copy in outs:
        copy.wait()


def pack_rows(arrays, parts, chunk, chunks, after=()):
    tokens, width = arrays[0].shape
    cut = width // parts // chunks
    kinds = len(arrays)

    def kernel(*refs):
        ins, (out, buffer, sems) = refs[:kinds], refs[-3:]
        pairs = [
            (ins[i].at[:, pl.ds((s * chunks + chunk) * cut, cut)], out.at[s, i])
            for s in range(parts)
            for i in range(kinds)
        ]
        move_pieces(pairs, buffer, sems)

    return pl.pallas_call(
        kernel,
        in_specs=[pl.BlockSpec(memory_space=pl.ANY)] * (kinds + len(after)),
        out_specs=pl.BlockSpec(memory_space=pl.ANY),
        out_shape=jax.ShapeDtypeStruct((parts, kinds, tokens, cut), BF),
        scratch_shapes=[
            pltpu.VMEM((parts * kinds, tokens, cut), BF),
            pltpu.SemaphoreType.DMA((2, parts * kinds)),
        ],
        cost_estimate=pl.CostEstimate(flops=0, bytes_accessed=0, transcendentals=0),
        name="pack_rows",
    )(*arrays, *after)


def unpack_rows(packed, chunk, chunks, before, after=()):
    parts, kinds, tokens, cut = packed.shape
    before = before or []

    def kernel(*refs):
        ref, outs, (buffer, sems) = refs[0], refs[-2 - kinds : -2], refs[-2:]
        pairs = [
            (ref.at[s, i], outs[i].at[:, pl.ds((s * chunks + chunk) * cut, cut)])
            for s in range(parts)
            for i in range(kinds)
        ]
        move_pieces(pairs, buffer, sems)

    return pl.pallas_call(
        kernel,
        in_specs=[pl.BlockSpec(memory_space=pl.ANY)] * (1 + len(before) + len(after)),
        out_specs=[pl.BlockSpec(memory_space=pl.ANY)] * kinds,
        out_shape=[jax.ShapeDtypeStruct((tokens, parts * chunks * cut), BF)] * kinds,
        scratch_shapes=[
            pltpu.VMEM((parts * kinds, tokens, cut), BF),
            pltpu.SemaphoreType.DMA((2, parts * kinds)),
        ],
        input_output_aliases={1 + i: i for i in range(len(before))},
        cost_estimate=pl.CostEstimate(flops=0, bytes_accessed=0, transcendentals=0),
        name="unpack_rows",
    )(packed, *before, *after)


def join_slabs(slabs, groups):
    rows, columns = slabs[0].shape
    count = len(slabs)
    pieces = [(g, n) for g, (first, end) in enumerate(groups) for n in range(first, end)]

    def kernel(*refs):
        ins, outs, (buffer, sems) = refs[:count], refs[count:-2], refs[-2:]
        arrive = [pltpu.make_async_copy(ins[n], buffer.at[n], sems.at[0, n]) for n in range(count)]
        leave = [
            pltpu.make_async_copy(buffer.at[n], outs[g].at[n - groups[g][0]], sems.at[1, m])
            for m, (g, n) in enumerate(pieces)
        ]
        for copy in arrive:
            copy.start()
        for copy in arrive:
            copy.wait()
        for copy in leave:
            copy.start()
        for copy in leave:
            copy.wait()

    return pl.pallas_call(
        kernel,
        in_specs=[pl.BlockSpec(memory_space=pl.ANY)] * count,
        out_specs=[pl.BlockSpec(memory_space=pl.ANY)] * len(groups),
        out_shape=[jax.ShapeDtypeStruct((end - first, rows, columns), BF) for first, end in groups],
        scratch_shapes=[
            pltpu.VMEM((count, rows, columns), BF),
            pltpu.SemaphoreType.DMA((2, max(count, len(pieces)))),
        ],
        cost_estimate=pl.CostEstimate(flops=0, bytes_accessed=0, transcendentals=0),
        name="join_slabs",
    )(*slabs)


def hold(array, after):
    def kernel(*refs):
        pass

    return pl.pallas_call(
        kernel,
        in_specs=[pl.BlockSpec(memory_space=pl.ANY)] * (1 + len(after)),
        out_specs=pl.BlockSpec(memory_space=pl.ANY),
        out_shape=jax.ShapeDtypeStruct(array.shape, array.dtype),
        input_output_aliases={0: 0},
        name="hold",
    )(array, *after)


def turn(array, after=()):
    tokens, width = array.shape
    step = width // 2

    def kernel(*refs):
        refs[-1][...] = refs[0][...].T

    return pl.pallas_call(
        kernel,
        grid=(width // step,),
        in_specs=[pl.BlockSpec((tokens, step), lambda i: (0, i))]
        + [pl.BlockSpec(memory_space=pl.ANY)] * len(after),
        out_specs=pl.BlockSpec((step, tokens), lambda i: (i, 0)),
        out_shape=jax.ShapeDtypeStruct((width, tokens), BF),
        name="turn_layer_input",
    )(array, *after)


def attention(items, bias, after=()):
    blocks, _, _, width = items.shape
    heads = width // HDIM
    tokens = blocks * BLK
    pair = 2 * BLK
    factor = HDIM ** (-0.5)
    nt = (((1,), (1,)), ((), ()))

    def kernel(*refs):
        items_ref, bias_ref = refs[:2]
        out_ref, key_sum, value_sum = refs[-3:]
        for h in range(heads):
            cols = slice(h * HDIM, (h + 1) * HDIM)
            keys = items_ref[:, 1, :, cols].reshape(tokens, HDIM)
            values = items_ref[:, 2, :, cols].reshape(tokens, HDIM)
            keys_t = keys.T
            key_sum[...] = jnp.zeros_like(key_sum)
            value_sum[...] = jnp.zeros_like(value_sum)

            def step(n, _):
                query = items_ref[pl.ds(2 * n, 2), 0, :, cols].reshape(pair, HDIM)
                grad = items_ref[pl.ds(2 * n, 2), 3, :, cols].reshape(pair, HDIM)
                scores = lax.dot_general(keys, query, nt, preferred_element_type=F32)
                near = bias_ref[n]
                scores = (
                    scores.reshape(blocks, BLK, pair) * (factor * math.log2(math.e)) + near[:, None, :]
                ).reshape(tokens, pair)
                top = jnp.max(scores, axis=0, keepdims=True)
                weights = jnp.exp2(scores - top)
                prob_grad = lax.dot_general(values, grad, nt, preferred_element_type=F32)
                inverse = 1.0 / jnp.sum(weights, axis=0, keepdims=True)
                row_dot = jnp.sum(weights * prob_grad, axis=0, keepdims=True) * inverse
                probs = weights * inverse
                probs_low = probs.astype(BF)
                score_grad = (probs * (prob_grad - row_dot)).astype(BF)
                value_sum[...] += jnp.dot(probs_low, grad, preferred_element_type=F32)
                key_sum[...] += jnp.dot(score_grad, query, preferred_element_type=F32)
                query_grad_t = jnp.dot(keys_t, score_grad, preferred_element_type=F32) * factor
                out_ref[pl.ds(2 * n, 2), 0, :, cols] = query_grad_t.T.astype(BF).reshape(2, BLK, HDIM)
                return 0

            lax.fori_loop(0, blocks // 2, step, 0)
            out_ref[:, 1, :, cols] = (key_sum[...] * factor).astype(BF).reshape(blocks, BLK, HDIM)
            out_ref[:, 2, :, cols] = value_sum[...].astype(BF).reshape(blocks, BLK, HDIM)

    return pl.pallas_call(
        kernel,
        in_specs=[pl.BlockSpec(memory_space=pltpu.VMEM)] * 2 + [pl.BlockSpec(memory_space=pl.ANY)] * len(after),
        out_specs=pl.BlockSpec(memory_space=pltpu.VMEM),
        out_shape=jax.ShapeDtypeStruct((blocks, 3, BLK, width), BF),
        scratch_shapes=[pltpu.VMEM((tokens, HDIM), F32), pltpu.VMEM((tokens, HDIM), F32)],
        compiler_params=pltpu.CompilerParams(vmem_limit_bytes=40 * MIB),
        cost_estimate=pl.CostEstimate(flops=0, bytes_accessed=0, transcendentals=0),
        name="attention_backward",
    )(items, bias, *after)


def weight_products(units, places, grads, chunk, chunks, norm, before):
    blocks, snaps = len(units), len(grads)
    rows = units[0][0][0].shape[1]
    cut = grads[0].shape[-1]
    group = 4
    steps = 4
    row_step = rows // steps
    before = [] if before is None else [before]
    flat = [piece for unit in units for piece, _ in unit]
    spots, at = [], 0
    for unit in units:
        spot = {}
        for piece, snap in unit:
            spot.update({snap + i: (at, i) for i in range(piece.shape[0])})
            at += 1
        spots.append(spot)

    def kernel(*refs):
        places_ref, unit_refs = refs[0], refs[1 : 1 + len(flat)]
        grad_refs, out_ref = refs[1 + len(flat) : 1 + len(flat) + snaps], refs[-1]
        for start in range(0, blocks, group):
            for k in range(snaps):
                here = [u for u in range(start, min(start + group, blocks)) if k in spots[u]]
                near = [spots[u][k] for u in here]
                left = jnp.concatenate([unit_refs[n][i] for n, i in near], axis=1)
                for kind in range(3):
                    right = jnp.concatenate([grad_refs[k][places_ref[u], kind] for u in here], axis=0)
                    part = jnp.dot(left, right, preferred_element_type=F32)
                    if start > 0 or k > 0:
                        part = out_ref[kind] + part
                    out_ref[kind] = part * norm if start + group >= blocks and k == snaps - 1 else part

    return pl.pallas_call(
        kernel,
        grid_spec=pltpu.PrefetchScalarGridSpec(
            num_scalar_prefetch=1,
            grid=(steps,),
            in_specs=[pl.BlockSpec((a.shape[0], row_step, BLK), lambda r, _: (0, r, 0)) for a in flat]
            + [pl.BlockSpec((blocks, 3, BLK, cut), lambda r, _: (0, 0, 0, 0))] * snaps
            + [pl.BlockSpec(memory_space=pl.ANY)] * len(before),
            out_specs=pl.BlockSpec((3, row_step, cut), lambda r, _: (0, r, chunk)),
        ),
        out_shape=jax.ShapeDtypeStruct((3, rows, chunks * cut), F32),
        input_output_aliases={1 + len(flat) + snaps: 0} if before else {},
        compiler_params=pltpu.CompilerParams(vmem_limit_bytes=56 * MIB),
        cost_estimate=pl.CostEstimate(flops=0, bytes_accessed=0, transcendentals=0),
        name="weight_products",
    )(places, *flat, *grads, *before)


def add_products(pieces, places, grads, norm, total):
    chunks, cut = len(grads[0]), grads[0][0].shape[-1]
    _, rows, columns = total.shape
    steps = 4
    row_step = rows // steps
    needed = [(u, n, i, snap + i) for n, (u, piece, snap) in enumerate(pieces) for i in range(piece.shape[0])]

    def kernel(*refs):
        piece_refs, grad_refs = refs[1 : 1 + len(pieces)], refs[1 + len(pieces) : -2]
        total_ref, out_ref = refs[-2:]
        left = jnp.concatenate([piece_refs[n][i] for _, n, i, _ in needed], axis=1)
        for c in range(chunks):
            for kind in range(3):
                right = jnp.concatenate([grad_refs[m * chunks + c][0, kind] for m in range(len(needed))], axis=0)
                part = jnp.dot(left, right, preferred_element_type=F32)
                cols = slice(c * cut, (c + 1) * cut)
                out_ref[kind, :, cols] = (total_ref[kind, :, cols] + part) * norm

    def block_of(u):
        return pl.BlockSpec((1, 3, BLK, cut), lambda r, places_ref: (places_ref[u], 0, 0, 0))

    whole = pl.BlockSpec((3, row_step, columns), lambda r, _: (0, r, 0))
    return pl.pallas_call(
        kernel,
        grid_spec=pltpu.PrefetchScalarGridSpec(
            num_scalar_prefetch=1,
            grid=(steps,),
            in_specs=[pl.BlockSpec((p.shape[0], row_step, BLK), lambda r, _: (0, r, 0)) for _, p, _ in pieces]
            + [block_of(u) for u, _, _, _ in needed for _ in range(chunks)]
            + [whole],
            out_specs=whole,
        ),
        out_shape=jax.ShapeDtypeStruct(total.shape, F32),
        input_output_aliases={1 + len(pieces) + len(needed) * chunks: 0},
        compiler_params=pltpu.CompilerParams(vmem_limit_bytes=32 * MIB),
        cost_estimate=pl.CostEstimate(flops=0, bytes_accessed=0, transcendentals=0),
        name="add_products",
    )(places, *[p for _, p, _ in pieces], *[g for _, _, _, k in needed for g in grads[k]], total)


def seq_swap(array, bit):
    return lax.ppermute(array, "seq", [(i, i ^ bit) for i in range(lax.axis_size("seq"))])


def local(layer_input, query_rows, key_rows, value_rows, out_grad, neighbours, counts):
    seq_count = lax.axis_size("seq")
    dp_count = lax.axis_size("dp")
    here = lax.axis_index("dp")
    width = query_rows.shape[2]
    heads_here = width // seq_count // HDIM
    blocks = neighbours.shape[1]
    chunks = 2 if heads_here % 2 == 0 else 1
    rows_here = layer_input.shape[2] // dp_count
    y_count = dp_count // 2

    def peer(p, j, e):
        return ((p // 2 + j) % y_count) * 2 + ((p % 2) ^ e)

    peers = [(j, e) for j in range(y_count) for e in range(2)]

    def dp_move(array, j, e):
        return lax.ppermute(array, "dp", [(peer(p, j, e), p) for p in range(dp_count)])

    rows_in = [query_rows[0], key_rows[0], value_rows[0], out_grad[0]]
    live = jnp.arange(neighbours.shape[2])[None, :] < counts[0][:, None]
    hit = (neighbours[0][:, :, None] == jnp.arange(blocks)[None, None, :]) & live[:, :, None]
    near = jnp.where(jnp.any(hit, axis=1), 0.0, -jnp.inf).astype(F32)
    bias = jnp.repeat(near.reshape(blocks // 2, 2, blocks).transpose(0, 2, 1), BLK, axis=2)

    packed = [pack_rows(rows_in, seq_count, 0, chunks)]
    items = [lax.all_to_all(packed[0], "seq", 0, 0, tiled=True)]

    turned = turn(layer_input[0], packed)
    slabs = []
    for j, e in peers:
        to = peer(here, (y_count - j) % y_count, e)
        slab = lax.dynamic_slice_in_dim(turned, to * rows_here, rows_here, 0)
        slabs.append(slab if (j, e) == (0, 0) else dp_move(slab, j, e))
    packed += [pack_rows(rows_in, seq_count, c, chunks, [turned]) for c in range(1, chunks)]
    middle = 3 * dp_count // 4
    own, *own_halves = join_slabs(slabs, [(0, dp_count), (0, middle), (middle, dp_count)])
    at = lax.axis_index("seq")
    ready, behind = [[] for _ in range(chunks)], [[], []]
    if seq_count == 8:
        units = {0: [own]}
        for bits, source, step in ((2, 0, 2), (4, 0, 4), (6, 4, 2), (1, 0, 1), (3, 2, 1), (5, 4, 1), (7, 6, 1)):
            pieces = own_halves if source == 0 and bits in HALVED else units[source]
            units[bits] = [seq_swap(a, step) for a in pieces]
        for c in range(1, chunks):
            packed[c] = hold(packed[c], [units[n][h] for n, h in HOLD_1])
        ready[0] = packed[1:2]
        behind = [[units[n][h] for n, h in HOLD_2], [units[n][h] for n, h in HOLD_3]]
        places = jnp.stack([at ^ bits for bits in units]).astype(jnp.int32)
        late = [(list(units).index(n), units[n][h], h * middle) for n, h in LATE]
        units = [
            [(a, h * middle) for h, a in enumerate(halves) if (n, h) not in LATE]
            for n, halves in units.items()
        ]
    else:
        every = [lax.all_gather(half, "seq", axis=0, tiled=False) for half in own_halves]
        units = [[(half[i], h * middle) for h, half in enumerate(every)] for i in range(seq_count)]
        late = []
        places = jnp.arange(seq_count, dtype=jnp.int32)
    items += [lax.all_to_all(a, "seq", 0, 0, tiled=True) for a in packed[1:]]

    norm = 1.0 / math.sqrt(neighbours.shape[1] * BLK * dp_count)
    weight_grad, backs, every_grad = None, [], []
    for c in range(chunks):
        out = attention(items[c], bias, ready[c])
        over_y = [out] + [dp_move(out, j, 0) for j in range(1, y_count)]
        grads = [a for there in over_y for a in (there, dp_move(there, 0, 1))]
        wait = behind[c] + (over_y[1:] if c == 0 else [])
        if c == 1 and EARLY:
            wait = wait + [weight_grad]
        back = hold(out, wait) if wait and chunks == 2 else out
        backs.append(lax.all_to_all(back, "seq", 0, 0, tiled=True))
        weight_grad = weight_products(units, places, grads, c, chunks, 1.0 if late else norm, weight_grad)
        every_grad.append(grads)
    if late:
        weight_grad = add_products(late, places, list(zip(*every_grad)), norm, weight_grad)
    done = None
    for c in range(chunks):
        done = unpack_rows(backs[c], c, chunks, done, [weight_grad] if c == chunks - 1 else [])
    query_grad, key_grad, value_grad = done
    return query_grad[None], key_grad[None], value_grad[None], weight_grad


def solution(mesh):
    placed = (P("dp", "seq", None),) * 5 + (P("dp", None, None), P("dp", None))
    return jax.shard_map(
        local,
        mesh=mesh,
        in_specs=placed,
        out_specs=(P("dp", "seq", None),) * 3 + (P(None, "dp", "seq"),),
        check_vma=False,
    )
```

```python
import math

import jax
import jax.numpy as jnp
from jax import lax
from jax.experimental import pallas as pl
from jax.experimental.pallas import tpu as pltpu
from jax.sharding import PartitionSpec as P

HDIM = 128
BLK = 128
MIB = 1 << 20
BF = jnp.bfloat16
F32 = jnp.float32
HOLD_1 = [(2, 0), (2, 1), (4, 0), (4, 1), (1, 0), (3, 0), (3, 1)]
HOLD_2 = [(6, 0), (5, 0), (5, 1)]
HOLD_3 = [(6, 1), (7, 0)]
LATE = [(6, 1), (7, 0), (7, 1)]
EARLY = True
HALVED = (2, 4)


def move_pieces(pairs, buffer, sems):
    ins = [pltpu.make_async_copy(a, buffer.at[n], sems.at[0, n]) for n, (a, _) in enumerate(pairs)]
    outs = [pltpu.make_async_copy(buffer.at[n], b, sems.at[1, n]) for n, (_, b) in enumerate(pairs)]
    for copy in ins:
        copy.start()
    for copy, then in zip(ins, outs):
        copy.wait()
        then.start()
    for copy in outs:
        copy.wait()


def pack_rows(arrays, parts, chunk, chunks, after=()):
    tokens, width = arrays[0].shape
    cut = width // parts // chunks
    kinds = len(arrays)

    def kernel(*refs):
        ins, (out, buffer, sems) = refs[:kinds], refs[-3:]
        pairs = [
            (ins[i].at[:, pl.ds((s * chunks + chunk) * cut, cut)], out.at[s, i])
            for s in range(parts)
            for i in range(kinds)
        ]
        move_pieces(pairs, buffer, sems)

    return pl.pallas_call(
        kernel,
        in_specs=[pl.BlockSpec(memory_space=pl.ANY)] * (kinds + len(after)),
        out_specs=pl.BlockSpec(memory_space=pl.ANY),
        out_shape=jax.ShapeDtypeStruct((parts, kinds, tokens, cut), BF),
        scratch_shapes=[
            pltpu.VMEM((parts * kinds, tokens, cut), BF),
            pltpu.SemaphoreType.DMA((2, parts * kinds)),
        ],
        cost_estimate=pl.CostEstimate(flops=0, bytes_accessed=0, transcendentals=0),
        name="pack_rows",
    )(*arrays, *after)


def unpack_rows(packed, chunk, chunks, before, after=()):
    parts, kinds, tokens, cut = packed.shape
    before = before or []

    def kernel(*refs):
        ref, outs, (buffer, sems) = refs[0], refs[-2 - kinds : -2], refs[-2:]
        pairs = [
            (ref.at[s, i], outs[i].at[:, pl.ds((s * chunks + chunk) * cut, cut)])
            for s in range(parts)
            for i in range(kinds)
        ]
        move_pieces(pairs, buffer, sems)

    return pl.pallas_call(
        kernel,
        in_specs=[pl.BlockSpec(memory_space=pl.ANY)] * (1 + len(before) + len(after)),
        out_specs=[pl.BlockSpec(memory_space=pl.ANY)] * kinds,
        out_shape=[jax.ShapeDtypeStruct((tokens, parts * chunks * cut), BF)] * kinds,
        scratch_shapes=[
            pltpu.VMEM((parts * kinds, tokens, cut), BF),
            pltpu.SemaphoreType.DMA((2, parts * kinds)),
        ],
        input_output_aliases={1 + i: i for i in range(len(before))},
        cost_estimate=pl.CostEstimate(flops=0, bytes_accessed=0, transcendentals=0),
        name="unpack_rows",
    )(packed, *before, *after)


def join_slabs(slabs, groups):
    rows, columns = slabs[0].shape
    count = len(slabs)
    pieces = [(g, n) for g, (first, end) in enumerate(groups) for n in range(first, end)]

    def kernel(*refs):
        ins, outs, (buffer, sems) = refs[:count], refs[count:-2], refs[-2:]
        arrive = [pltpu.make_async_copy(ins[n], buffer.at[n], sems.at[0, n]) for n in range(count)]
        leave = [
            pltpu.make_async_copy(buffer.at[n], outs[g].at[n - groups[g][0]], sems.at[1, m])
            for m, (g, n) in enumerate(pieces)
        ]
        for copy in arrive:
            copy.start()
        for copy in arrive:
            copy.wait()
        for copy in leave:
            copy.start()
        for copy in leave:
            copy.wait()

    return pl.pallas_call(
        kernel,
        in_specs=[pl.BlockSpec(memory_space=pl.ANY)] * count,
        out_specs=[pl.BlockSpec(memory_space=pl.ANY)] * len(groups),
        out_shape=[jax.ShapeDtypeStruct((end - first, rows, columns), BF) for first, end in groups],
        scratch_shapes=[
            pltpu.VMEM((count, rows, columns), BF),
            pltpu.SemaphoreType.DMA((2, max(count, len(pieces)))),
        ],
        cost_estimate=pl.CostEstimate(flops=0, bytes_accessed=0, transcendentals=0),
        name="join_slabs",
    )(*slabs)


def hold(array, after):
    def kernel(*refs):
        pass

    return pl.pallas_call(
        kernel,
        in_specs=[pl.BlockSpec(memory_space=pl.ANY)] * (1 + len(after)),
        out_specs=pl.BlockSpec(memory_space=pl.ANY),
        out_shape=jax.ShapeDtypeStruct(array.shape, array.dtype),
        input_output_aliases={0: 0},
        name="hold",
    )(array, *after)


def turn(array, after=()):
    tokens, width = array.shape
    step = width // 2

    def kernel(*refs):
        refs[-1][...] = refs[0][...].T

    return pl.pallas_call(
        kernel,
        grid=(width // step,),
        in_specs=[pl.BlockSpec((tokens, step), lambda i: (0, i))]
        + [pl.BlockSpec(memory_space=pl.ANY)] * len(after),
        out_specs=pl.BlockSpec((step, tokens), lambda i: (i, 0)),
        out_shape=jax.ShapeDtypeStruct((width, tokens), BF),
        name="turn_layer_input",
    )(array, *after)


def attention(items, bias, after=()):
    blocks, _, _, width = items.shape
    heads = width // HDIM
    tokens = blocks * BLK
    pair = 2 * BLK
    factor = HDIM ** (-0.5)
    nt = (((1,), (1,)), ((), ()))

    def kernel(*refs):
        items_ref, bias_ref = refs[:2]
        out_ref, key_sum, value_sum = refs[-3:]
        for h in range(heads):
            cols = slice(h * HDIM, (h + 1) * HDIM)
            keys = items_ref[:, 1, :, cols].reshape(tokens, HDIM)
            values = items_ref[:, 2, :, cols].reshape(tokens, HDIM)
            keys_t = keys.T
            key_sum[...] = jnp.zeros_like(key_sum)
            value_sum[...] = jnp.zeros_like(value_sum)

            def step(n, _):
                query = items_ref[pl.ds(2 * n, 2), 0, :, cols].reshape(pair, HDIM)
                grad = items_ref[pl.ds(2 * n, 2), 3, :, cols].reshape(pair, HDIM)
                scores = lax.dot_general(keys, query, nt, preferred_element_type=F32)
                near = bias_ref[n]
                scores = (
                    scores.reshape(blocks, BLK, pair) * (factor * math.log2(math.e)) + near[:, None, :]
                ).reshape(tokens, pair)
                top = jnp.max(scores, axis=0, keepdims=True)
                weights = jnp.exp2(scores - top)
                prob_grad = lax.dot_general(values, grad, nt, preferred_element_type=F32)
                inverse = 1.0 / jnp.sum(weights, axis=0, keepdims=True)
                row_dot = jnp.sum(weights * prob_grad, axis=0, keepdims=True) * inverse
                probs = weights * inverse
                probs_low = probs.astype(BF)
                score_grad = (probs * (prob_grad - row_dot)).astype(BF)
                value_sum[...] += jnp.dot(probs_low, grad, preferred_element_type=F32)
                key_sum[...] += jnp.dot(score_grad, query, preferred_element_type=F32)
                query_grad_t = jnp.dot(keys_t, score_grad, preferred_element_type=F32) * factor
                out_ref[pl.ds(2 * n, 2), 0, :, cols] = query_grad_t.T.astype(BF).reshape(2, BLK, HDIM)
                return 0

            lax.fori_loop(0, blocks // 2, step, 0)
            out_ref[:, 1, :, cols] = (key_sum[...] * factor).astype(BF).reshape(blocks, BLK, HDIM)
            out_ref[:, 2, :, cols] = value_sum[...].astype(BF).reshape(blocks, BLK, HDIM)

    return pl.pallas_call(
        kernel,
        in_specs=[pl.BlockSpec(memory_space=pltpu.VMEM)] * 2 + [pl.BlockSpec(memory_space=pl.ANY)] * len(after),
        out_specs=pl.BlockSpec(memory_space=pltpu.VMEM),
        out_shape=jax.ShapeDtypeStruct((blocks, 3, BLK, width), BF),
        scratch_shapes=[pltpu.VMEM((tokens, HDIM), F32), pltpu.VMEM((tokens, HDIM), F32)],
        compiler_params=pltpu.CompilerParams(vmem_limit_bytes=40 * MIB),
        cost_estimate=pl.CostEstimate(flops=0, bytes_accessed=0, transcendentals=0),
        name="attention_backward",
    )(items, bias, *after)


def weight_products(units, places, grads, chunk, chunks, norm, before):
    blocks, snaps = len(units), len(grads)
    rows = units[0][0][0].shape[1]
    cut = grads[0].shape[-1]
    group = 4
    steps = 4
    row_step = rows // steps
    before = [] if before is None else [before]
    flat = [piece for unit in units for piece, _ in unit]
    spots, at = [], 0
    for unit in units:
        spot = {}
        for piece, snap in unit:
            spot.update({snap + i: (at, i) for i in range(piece.shape[0])})
            at += 1
        spots.append(spot)

    def kernel(*refs):
        places_ref, unit_refs = refs[0], refs[1 : 1 + len(flat)]
        grad_refs, out_ref = refs[1 + len(flat) : 1 + len(flat) + snaps], refs[-1]
        for start in range(0, blocks, group):
            for k in range(snaps):
                here = [u for u in range(start, min(start + group, blocks)) if k in spots[u]]
                near = [spots[u][k] for u in here]
                left = jnp.concatenate([unit_refs[n][i] for n, i in near], axis=1)
                for kind in range(3):
                    right = jnp.concatenate([grad_refs[k][places_ref[u], kind] for u in here], axis=0)
                    part = jnp.dot(left, right, preferred_element_type=F32)
                    if start > 0 or k > 0:
                        part = out_ref[kind] + part
                    out_ref[kind] = part * norm if start + group >= blocks and k == snaps - 1 else part

    return pl.pallas_call(
        kernel,
        grid_spec=pltpu.PrefetchScalarGridSpec(
            num_scalar_prefetch=1,
            grid=(steps,),
            in_specs=[pl.BlockSpec((a.shape[0], row_step, BLK), lambda r, _: (0, r, 0)) for a in flat]
            + [pl.BlockSpec((blocks, 3, BLK, cut), lambda r, _: (0, 0, 0, 0))] * snaps
            + [pl.BlockSpec(memory_space=pl.ANY)] * len(before),
            out_specs=pl.BlockSpec((3, row_step, cut), lambda r, _: (0, r, chunk)),
        ),
        out_shape=jax.ShapeDtypeStruct((3, rows, chunks * cut), F32),
        input_output_aliases={1 + len(flat) + snaps: 0} if before else {},
        compiler_params=pltpu.CompilerParams(vmem_limit_bytes=62 * MIB),
        cost_estimate=pl.CostEstimate(flops=0, bytes_accessed=0, transcendentals=0),
        name="weight_products",
    )(places, *flat, *grads, *before)


def add_products(pieces, places, grads, norm, total):
    chunks, cut = len(grads[0]), grads[0][0].shape[-1]
    _, rows, columns = total.shape
    steps = 2
    row_step = rows // steps
    needed = [(u, n, i, snap + i) for n, (u, piece, snap) in enumerate(pieces) for i in range(piece.shape[0])]

    def kernel(*refs):
        piece_refs, grad_refs = refs[1 : 1 + len(pieces)], refs[1 + len(pieces) : -2]
        total_ref, out_ref = refs[-2:]
        left = jnp.concatenate([piece_refs[n][i] for _, n, i, _ in needed], axis=1)
        for c in range(chunks):
            for kind in range(3):
                right = jnp.concatenate([grad_refs[m * chunks + c][0, kind] for m in range(len(needed))], axis=0)
                part = jnp.dot(left, right, preferred_element_type=F32)
                cols = slice(c * cut, (c + 1) * cut)
                out_ref[kind, :, cols] = (total_ref[kind, :, cols] + part) * norm

    def block_of(u):
        return pl.BlockSpec((1, 3, BLK, cut), lambda r, places_ref: (places_ref[u], 0, 0, 0))

    whole = pl.BlockSpec((3, row_step, columns), lambda r, _: (0, r, 0))
    return pl.pallas_call(
        kernel,
        grid_spec=pltpu.PrefetchScalarGridSpec(
            num_scalar_prefetch=1,
            grid=(steps,),
            in_specs=[pl.BlockSpec((p.shape[0], row_step, BLK), lambda r, _: (0, r, 0)) for _, p, _ in pieces]
            + [block_of(u) for u, _, _, _ in needed for _ in range(chunks)]
            + [whole],
            out_specs=whole,
        ),
        out_shape=jax.ShapeDtypeStruct(total.shape, F32),
        input_output_aliases={1 + len(pieces) + len(needed) * chunks: 0},
        compiler_params=pltpu.CompilerParams(vmem_limit_bytes=62 * MIB),
        cost_estimate=pl.CostEstimate(flops=0, bytes_accessed=0, transcendentals=0),
        name="add_products",
    )(places, *[p for _, p, _ in pieces], *[g for _, _, _, k in needed for g in grads[k]], total)


def seq_swap(array, bit):
    return lax.ppermute(array, "seq", [(i, i ^ bit) for i in range(lax.axis_size("seq"))])


def local(layer_input, query_rows, key_rows, value_rows, out_grad, neighbours, counts):
    seq_count = lax.axis_size("seq")
    dp_count = lax.axis_size("dp")
    here = lax.axis_index("dp")
    width = query_rows.shape[2]
    heads_here = width // seq_count // HDIM
    blocks = neighbours.shape[1]
    chunks = 2 if heads_here % 2 == 0 else 1
    rows_here = layer_input.shape[2] // dp_count
    y_count = dp_count // 2

    def peer(p, j, e):
        return ((p // 2 + j) % y_count) * 2 + ((p % 2) ^ e)

    peers = [(j, e) for j in range(y_count) for e in range(2)]

    def dp_move(array, j, e):
        return lax.ppermute(array, "dp", [(peer(p, j, e), p) for p in range(dp_count)])

    rows_in = [query_rows[0], key_rows[0], value_rows[0], out_grad[0]]
    live = jnp.arange(neighbours.shape[2])[None, :] < counts[0][:, None]
    hit = (neighbours[0][:, :, None] == jnp.arange(blocks)[None, None, :]) & live[:, :, None]
    near = jnp.where(jnp.any(hit, axis=1), 0.0, -jnp.inf).astype(F32)
    bias = jnp.repeat(near.reshape(blocks // 2, 2, blocks).transpose(0, 2, 1), BLK, axis=2)

    packed = [pack_rows(rows_in, seq_count, 0, chunks)]
    items = [lax.all_to_all(packed[0], "seq", 0, 0, tiled=True)]

    turned = turn(layer_input[0], packed)
    slabs = []
    for j, e in peers:
        to = peer(here, (y_count - j) % y_count, e)
        slab = lax.dynamic_slice_in_dim(turned, to * rows_here, rows_here, 0)
        slabs.append(slab if (j, e) == (0, 0) else dp_move(slab, j, e))
    packed += [pack_rows(rows_in, seq_count, c, chunks, [turned]) for c in range(1, chunks)]
    middle = 3 * dp_count // 4
    own, *own_halves = join_slabs(slabs, [(0, dp_count), (0, middle), (middle, dp_count)])
    at = lax.axis_index("seq")
    ready, behind = [[] for _ in range(chunks)], [[], []]
    if seq_count == 8:
        units = {0: [own]}
        for bits, source, step in ((2, 0, 2), (4, 0, 4), (6, 4, 2), (1, 0, 1), (3, 2, 1), (5, 4, 1), (7, 6, 1)):
            pieces = own_halves if source == 0 and bits in HALVED else units[source]
            units[bits] = [seq_swap(a, step) for a in pieces]
        for c in range(1, chunks):
            packed[c] = hold(packed[c], [units[n][h] for n, h in HOLD_1])
        ready[0] = packed[1:2]
        behind = [[units[n][h] for n, h in HOLD_2], [units[n][h] for n, h in HOLD_3]]
        places = jnp.stack([at ^ bits for bits in units]).astype(jnp.int32)
        late = [(list(units).index(n), units[n][h], h * middle) for n, h in LATE]
        units = [
            [(a, h * middle) for h, a in enumerate(halves) if (n, h) not in LATE]
            for n, halves in units.items()
        ]
    else:
        every = [lax.all_gather(half, "seq", axis=0, tiled=False) for half in own_halves]
        units = [[(half[i], h * middle) for h, half in enumerate(every)] for i in range(seq_count)]
        late = []
        places = jnp.arange(seq_count, dtype=jnp.int32)
    items += [lax.all_to_all(a, "seq", 0, 0, tiled=True) for a in packed[1:]]

    norm = 1.0 / math.sqrt(neighbours.shape[1] * BLK * dp_count)
    weight_grad, backs, every_grad = None, [], []
    for c in range(chunks):
        out = attention(items[c], bias, ready[c])
        over_y = [out] + [dp_move(out, j, 0) for j in range(1, y_count)]
        grads = [a for there in over_y for a in (there, dp_move(there, 0, 1))]
        wait = behind[c] + (over_y[1:] if c == 0 else [])
        if c == 1 and EARLY:
            wait = wait + [weight_grad]
        back = hold(out, wait) if wait and chunks == 2 else out
        backs.append(lax.all_to_all(back, "seq", 0, 0, tiled=True))
        weight_grad = weight_products(units, places, grads, c, chunks, 1.0 if late else norm, weight_grad)
        every_grad.append(grads)
    if late:
        weight_grad = add_products(late, places, list(zip(*every_grad)), norm, weight_grad)
    done = None
    for c in range(chunks):
        done = unpack_rows(backs[c], c, chunks, done, [weight_grad] if c == chunks - 1 else [])
    query_grad, key_grad, value_grad = done
    return query_grad[None], key_grad[None], value_grad[None], weight_grad


def solution(mesh):
    placed = (P("dp", "seq", None),) * 5 + (P("dp", None, None), P("dp", None))
    return jax.shard_map(
        local,
        mesh=mesh,
        in_specs=placed,
        out_specs=(P("dp", "seq", None),) * 3 + (P(None, "dp", "seq"),),
        check_vma=False,
    )
```
